32 devices in a mesh: groups: 2 (over x), mem: 16 (over z, y, core).
Axes of the slice: x: 2, y: 2, z: 4, core: 2. Of those that a mesh axis runs over, the one named last changes fastest.
Arguments:
- mem_key: bfloat16 [128, 128, 128], P(('groups', 'mem')), parts along dimension 0, may hold values from -6 to 6
- value_base: bfloat16 [128, 128, 512], P(('groups', 'mem')), parts along dimension 0, may hold values from -6 to 6
- memory_labels: int32 [128, 128], P(('groups', 'mem')), parts along dimension 0, may hold values from 0 to 7
- valid_counts: int32 [32], P(('groups', 'mem')), parts along dimension 0, may hold values from 128 to 512, as said below
- query_key: bfloat16 [32, 64, 128], P(('groups', 'mem')), parts along dimension 0, may hold values from -96 to 96
- query_value: bfloat16 [32, 64, 512], P(('groups', 'mem')), parts along dimension 0, may hold values from -6 to 6
- object_embed: bfloat16 [8, 512], replicated, may hold values from -6 to 6
- decode_weight: bfloat16 [3, 3, 1024, 256], replicated, may hold values from -0.0625 to 0.0625
- mask_weight: bfloat16 [256, 8], replicated, may hold values from -0.375 to 0.375
Outputs:
- mask_logits: float32 [32, 64, 8], P(('groups', 'mem')), parts along dimension 0
The draws below stay inside these ranges and needn't reach their ends.
There are 2 independent parts, one for each index of `groups`. The reference program is written for one: setup_inputs(seed, part) draws one part's arguments, and reference() takes and returns one part's arrays. A program takes and returns all parts, laid end to end along the dimension named above; an argument that names none is the same for every part. Nothing has to cross between parts.
Inputs may be any that keep to these rules, and one draw needn't show every extreme that they name: `valid_counts`: live positions of each memory block; some block is full and some holds a quarter.
All inputs are finite; a program needn't handle non-finite values.
Results may differ from the reference program's by a relative error of at most 0.0048.
Values may be sent and summed in bfloat16 or wider, within the bound.
A program may use at most 320 MiB of HBM per device.

```python
import math
import jax
import jax.numpy as jnp
from jax import lax

KEY = 128
VAL = 512
DEC = 256
OBJ = 8
MCOLS = 128
QW = 64
MROWS = 4
MEM_ROWS = 64
QH = 16
N_MEM = 16


def draw_valid_counts(key, part):
    base_key = jax.random.fold_in(key, 11)
    first_key, second_key = jax.random.split(base_key)
    block_size = MROWS * MCOLS
    counts = jax.random.randint(first_key, (N_MEM,), block_size // 4, block_size + 1)
    order = jax.random.permutation(second_key, N_MEM)
    counts = counts.at[order[0]].set(block_size)
    counts = counts.at[order[1]].set(block_size // 4)
    return counts.astype(jnp.int32)


def draw_query_key(key, part):
    base_key = jax.random.fold_in(key, 23)
    first_key = jax.random.fold_in(base_key, 0)
    shape = (QH, QW, KEY)
    codes = jnp.clip(3.0 * jax.random.normal(first_key, shape, jnp.float32), -12.0, 12.0)
    return codes.astype(jnp.bfloat16)


def touch_ends(array, rng, low, top_value):
    shape = array.shape
    spot = [jax.random.randint(jax.random.fold_in(rng, axis), (), 0, shape[axis]) for axis in range(len(shape))]
    array = array.at[tuple(spot)].set(low)
    longest = shape.index(max(shape))
    spot[longest] = (spot[longest] + 1) % shape[longest]
    return array.at[tuple(spot)].set(top_value)


def shard_levels(stream_key, shape, pieces, least, high):
    loudness = 1.0
    for axis_at, blocks in pieces:
        heights = jax.random.uniform(jax.random.fold_in(jax.random.fold_in(stream_key, 6), axis_at), (blocks,), jnp.float32, least / len(pieces), high / len(pieces))
        loudness = loudness * jnp.repeat(jnp.exp(heights), shape[axis_at] // blocks).reshape((-1,) + (1,) * (len(shape) - 1 - axis_at))
    return loudness


def centred(key, shape, scale, bound, cuts=(), held_as=jnp.bfloat16):
    result = jax.random.normal(key, shape, jnp.float32) * scale
    if len(cuts) > 0:
        result = shard_levels(key, shape, cuts, -0.22, 0.18) * result
    return jnp.clip(result, min=-bound, max=bound).astype(held_as)


def setup_inputs(seed: int = 0, part: int = 0) -> dict:
    keys = jax.random.split(jax.random.key(seed), 10)
    part_keys = jax.random.split(jax.random.fold_in(keys[9], part), 10)
    return {
        "mem_key": centred(part_keys[0], (MEM_ROWS, MCOLS, KEY), 1.0, 6.0, ((0, 16),)),
        "value_base": centred(part_keys[1], (MEM_ROWS, MCOLS, VAL), 1.0, 6.0, ((0, 16),)),
        "memory_labels": touch_ends(jax.random.randint(part_keys[2], (MEM_ROWS, MCOLS), 0, OBJ), jax.random.fold_in(part_keys[2], 1), 0, OBJ - 1).astype(jnp.int32),
        "valid_counts": draw_valid_counts(jax.random.fold_in(jax.random.fold_in(keys[9], part), 71), part),
        "query_key": draw_query_key(jax.random.fold_in(jax.random.fold_in(keys[9], part), 71), part),
        "query_value": centred(part_keys[5], (QH, QW, VAL), 1.0, 6.0, ((0, 16),)),
        "object_embed": centred(keys[6], (OBJ, VAL), 1.0, 6.0),
        "decode_weight": centred(keys[7], (3, 3, 2 * VAL, DEC), (18 * VAL) ** -0.5, 0.0625),
        "mask_weight": centred(keys[8], (DEC, OBJ), DEC ** -0.5, 0.375),
    }


def conv_taps(padded, weight, height, width):
    summed = jnp.zeros((height * width, weight.shape[3]), jnp.float32)
    for row_step in range(3):
        for col_step in range(3):
            window = padded[row_step:row_step + height, col_step:col_step + width].reshape(height * width, -1)
            summed = summed + jnp.dot(window, weight[row_step, col_step], preferred_element_type=jnp.float32)
    return summed

def reference(mem_key, value_base, memory_labels, valid_counts, query_key, query_value, object_embed, decode_weight, mask_weight):
    block_size = MROWS * MCOLS
    onehot = (memory_labels.reshape(-1)[:, None] == jnp.arange(OBJ, dtype=jnp.int32)[None, :]).astype(jnp.bfloat16)
    embedded = jnp.dot(onehot, object_embed, preferred_element_type=jnp.float32)
    mem_value = (value_base.reshape(-1, VAL).astype(jnp.float32) + embedded).astype(jnp.bfloat16)
    keys_all = mem_key.reshape(N_MEM, block_size, KEY)
    mem_value = mem_value.reshape(N_MEM, block_size, VAL)
    queries = query_key.reshape(-1, KEY)
    score_scale = 1.0 / math.sqrt(KEY)

    def block(inputs):
        block_keys, block_vals, live_count = inputs
        scores = jnp.dot(queries, block_keys.T, preferred_element_type=jnp.float32) * score_scale
        is_live = (jnp.arange(block_size, dtype=jnp.int32) < live_count)[None, :]
        scores = jnp.where(is_live, scores, -jnp.inf)
        block_peak = lax.optimization_barrier(jnp.max(scores, axis=1))
        weights = jnp.where(is_live, jnp.exp(scores - block_peak[:, None]), 0.0).astype(jnp.bfloat16)
        block_mass = lax.optimization_barrier(jnp.sum(weights.astype(jnp.float32), axis=1))
        block_values = jnp.dot(weights, block_vals, preferred_element_type=jnp.float32)
        return (block_peak, block_mass, block_values)
    block_peak, block_mass, block_values = lax.map(block, (keys_all, mem_value, valid_counts))
    largest = lax.optimization_barrier(jnp.max(block_peak, axis=0))
    rescale = jnp.exp(block_peak - largest[None, :])
    weight_sum = lax.optimization_barrier(jnp.sum(rescale * block_mass, axis=0))
    value_sums = lax.optimization_barrier(jnp.sum(rescale[:, :, None] * block_values, axis=0))
    readout = (value_sums / weight_sum[:, None]).astype(jnp.bfloat16).reshape(QH, QW, VAL)
    joined = jnp.concatenate([readout, query_value], axis=-1)
    padded = jnp.pad(joined, ((1, 1), (1, 1), (0, 0)))
    hidden = jax.nn.relu(conv_taps(padded, decode_weight, QH, QW)).astype(jnp.bfloat16)
    logits = jnp.dot(hidden, mask_weight, preferred_element_type=jnp.float32)
    return logits.reshape(QH, QW, OBJ)
```

```python
import functools
import math

import jax
import jax.numpy as jnp
from jax import lax
from jax.experimental import pallas as pl
from jax.experimental.pallas import tpu as pltpu
from jax.sharding import PartitionSpec as P

F32 = jnp.float32
BF16 = jnp.bfloat16


def bit_xor(a, b, size):
    out, bit = 0, 1
    while bit < size:
        out = out + ((a // bit + b // bit) % 2) * bit
        bit *= 2
    return out


def remote(src, dst, send, recv, target):
    return pltpu.make_async_remote_copy(
        src_ref=src,
        dst_ref=dst,
        send_sem=send,
        recv_sem=recv,
        device_id={"mem": target},
        device_id_type=pl.DeviceIdType.MESH,
    )


def kernel(
    n,
    count_ref,
    keys_hbm,
    base_hbm,
    labels_hbm,
    query_hbm,
    qval_hbm,
    embed_hbm,
    weight_hbm,
    mask_hbm,
    out_ref,
    keys_ref,
    base_ref,
    labels_ref,
    query_ref,
    qval_ref,
    embed_ref,
    weight,
    mask_ref,
    load_sem,
    values,
    sib_keys,
    sib_values,
    bias,
    sib_bias,
    queries,
    send_vals,
    send_stats,
    recv_vals,
    recv_stats,
    halo_q,
    halo_r,
    readout,
    acc,
    sib_send,
    sib_recv,
    query_send,
    query_recv,
    vals_send,
    vals_recv,
    stats_send,
    stats_recv,
    haloq_send,
    haloq_recv,
    halor_send,
    halor_recv,
):
    chips = n // 2
    zs = chips // 2
    me = lax.axis_index("mem")
    core = me % 2
    chip = me // 2
    y = chip % 2
    z = chip // 2
    sibling = me + 1 - 2 * core
    other = me - 1 + 2 * core
    has_other = jnp.logical_and(other >= 0, other < n)
    width, val = qval_ref.shape
    scale = 1.0 / math.sqrt(keys_ref.shape[1])

    barrier = pltpu.get_barrier_semaphore()

    def greet(target):
        pl.semaphore_signal(
            barrier, inc=1, device_id={"mem": target}, device_id_type=pl.DeviceIdType.MESH
        )

    greet(sibling)
    for d in range(1, chips):
        greet(bit_xor(chip, d, chips) * 2 + core)

    @pl.when(has_other)
    def _():
        greet(other)

    loads = [
        pltpu.make_async_copy(src, dst, load_sem.at[k])
        for k, (src, dst) in enumerate(
            (
                (query_hbm, query_ref),
                (labels_hbm, labels_ref),
                (embed_hbm, embed_ref),
                (base_hbm, base_ref),
                (keys_hbm, keys_ref),
                (qval_hbm, qval_ref),
                (mask_hbm, mask_ref),
                (weight_hbm, weight),
            )
        )
    ]
    for load in loads:
        load.start()
    for load in loads[:4]:
        load.wait()

    objects = embed_ref.shape[0]
    embed = embed_ref[...].astype(F32)
    cols = labels_ref.shape[1]
    for row in range(labels_ref.shape[0]):
        lab = jnp.broadcast_to(labels_ref[row : row + 1, :], (objects, cols))
        onehot = (lab == lax.broadcasted_iota(jnp.int32, (objects, cols), 0)).astype(F32)
        added = lax.dot_general(
            onehot, embed, (((0,), (0,)), ((), ())), preferred_element_type=F32
        )
        part = pl.ds(row * cols, cols)
        values[part, :] = (base_ref[part, :].astype(F32) + added).astype(BF16)
    place = lax.broadcasted_iota(jnp.int32, bias.shape, 1)
    bias[...] = jnp.where(place < count_ref[0], 0.0, -jnp.inf).astype(F32)
    queries[chip] = query_ref[...]

    for load in loads[4:6]:
        load.wait()
    pl.semaphore_wait(barrier, chips + has_other.astype(jnp.int32))

    def query_copy(d):
        peer = bit_xor(chip, d, chips)
        send = remote(
            query_ref, queries.at[chip], query_send.at[peer], query_recv.at[chip], peer * 2 + core
        )
        recv = remote(
            query_ref, queries.at[peer], query_send.at[peer], query_recv.at[peer], peer * 2 + core
        )
        return send, recv

    for d in range(chips - 1, 0, -1):
        query_copy(d)[0].start()
    sib_copies = [
        remote(src, dst, sib_send.at[k], sib_recv.at[k], sibling)
        for k, (src, dst) in enumerate(
            ((keys_ref, sib_keys), (bias, sib_bias), (values, sib_values))
        )
    ]
    for copy in sib_copies:
        copy.start()

    def halo_copies(src, buf, send, recv):
        to_sib = remote(src, buf.at[core], send.at[0], recv.at[core], sibling)
        from_sib = remote(src, buf.at[1 - core], send.at[0], recv.at[1 - core], sibling)
        to_other = remote(src, buf.at[1 - core], send.at[1], recv.at[1 - core], other)
        from_other = remote(src, buf.at[core], send.at[1], recv.at[core], other)
        return to_sib, from_sib, to_other, from_other

    q_sib, q_from_sib, q_other, q_from_other = halo_copies(qval_ref, halo_q, haloq_send, haloq_recv)
    q_sib.start()

    @pl.when(has_other)
    def _():
        q_other.start()

    @pl.when(jnp.logical_not(has_other))
    def _():
        halo_q[core] = jnp.zeros((width, val), BF16)
        halo_r[core] = jnp.zeros((width, val), BF16)

    def wait_query(target_chip):
        remote(
            query_ref,
            queries.at[target_chip],
            query_send.at[target_chip],
            query_recv.at[target_chip],
            target_chip * 2 + core,
        ).wait_recv()

    def vals_copies(target):
        return (
            remote(
                send_vals.at[target],
                recv_vals.at[chip],
                vals_send.at[target],
                vals_recv.at[chip],
                target * 2 + core,
            ),
            remote(
                send_stats.at[target // 2],
                recv_stats.at[chip],
                stats_send.at[target],
                stats_recv.at[chip],
                target * 2 + core,
            ),
        )

    def step(k, carry):
        d = zs - 1 - k
        zt = bit_xor(z, d, zs)
        for yt in range(2):

            @pl.when(zt * 2 + yt != chip)
            def _():
                wait_query(zt * 2 + yt)

        @pl.when(k == 0)
        def _():
            for copy in sib_copies:
                copy.wait_recv()

        q = queries[pl.ds(zt * 2, 2)].reshape(2 * width, -1)
        contract = (((1,), (1,)), ((), ()))
        s0 = lax.dot_general(q, keys_ref[...], contract, preferred_element_type=F32)
        s1 = lax.dot_general(q, sib_keys[...], contract, preferred_element_type=F32)
        s0 = s0 * scale + bias[0:1, :]
        s1 = s1 * scale + sib_bias[0:1, :]
        peak = jnp.maximum(
            jnp.max(s0, axis=1, keepdims=True), jnp.max(s1, axis=1, keepdims=True)
        )
        w0 = jnp.exp(s0 - peak).astype(BF16)
        w1 = jnp.exp(s1 - peak).astype(BF16)
        mass = jnp.sum(w0.astype(F32) + w1.astype(F32), axis=1, keepdims=True)
        summed = jnp.dot(w0, values[...], preferred_element_type=F32) + jnp.dot(
            w1, sib_values[...], preferred_element_type=F32
        )
        send_vals[pl.ds(zt * 2, 2)] = summed.astype(BF16).reshape(2, width, val)
        lane = lax.broadcasted_iota(jnp.int32, (2 * width, 128), 1)
        stats = jnp.where(lane == 0, peak, mass)
        send_stats[zt] = stats.T[0:8, :]
        for yt in range(2):
            target = zt * 2 + yt

            @pl.when(target != chip)
            def _():
                for copy in vals_copies(target):
                    copy.start()

        return carry

    lax.fori_loop(0, zs, step, 0)
    recv_vals[chip] = send_vals[chip]
    recv_stats[chip] = send_stats[z]

    for load in loads[6:]:
        load.wait()
    q_from_sib.wait_recv()

    @pl.when(has_other)
    def _():
        q_from_other.wait_recv()

    for dc in range(3):
        total = jnp.zeros((width, acc.shape[2]), F32)
        for dr, src in enumerate((halo_q.at[0], qval_ref, halo_q.at[1])):
            total += jnp.dot(src[...], weight[dr, dc, val:, :], preferred_element_type=F32)
        acc[dc] = total

    for d in range(1, chips):
        peer = bit_xor(chip, d, chips)
        remote(
            send_vals.at[peer], recv_vals.at[peer], vals_send.at[peer], vals_recv.at[peer],
            peer * 2 + core,
        ).wait_recv()
        remote(
            send_stats.at[peer // 2], recv_stats.at[peer], stats_send.at[peer],
            stats_recv.at[peer], peer * 2 + core,
        ).wait_recv()

    peaks, masses = [], []
    for first in range(0, chips, 16):
        tiles = recv_stats[first : min(first + 16, chips)].reshape(-1, 2 * width)
        have = tiles.shape[0] // 8
        tiles = jnp.concatenate([tiles] * (16 // have), axis=0)
        turned = tiles.T
        turned = jnp.where(y == 0, turned[:width], turned[width:])
        for k in range(have):
            peaks.append(turned[:, k * 8 : k * 8 + 1])
            masses.append(turned[:, k * 8 + 1 : k * 8 + 2])
    largest = functools.reduce(jnp.maximum, peaks)
    weight_sum = jnp.zeros((width, 1), F32)
    value_sum = jnp.zeros((width, val), F32)
    for k in range(chips):
        factor = jnp.exp(peaks[k] - largest)
        weight_sum += factor * masses[k]
        value_sum += factor * recv_vals[k].astype(F32)
    readout[...] = (value_sum / weight_sum).astype(BF16)

    r_sib, r_from_sib, r_other, r_from_other = halo_copies(readout, halo_r, halor_send, halor_recv)

    @pl.when(has_other)
    def _():
        r_other.start()

    r_sib.start()
    for dc in range(3):
        acc[dc] += jnp.dot(readout[...], weight[1, dc, :val, :], preferred_element_type=F32)
    r_from_sib.wait_recv()

    @pl.when(has_other)
    def _():
        r_from_other.wait_recv()

    taps = []
    for dc in range(3):
        total = acc[dc]
        for dr, slot in ((0, 0), (2, 1)):
            total += jnp.dot(halo_r[slot], weight[dr, dc, :val, :], preferred_element_type=F32)
        taps.append(total)
    zero = jnp.zeros((1, acc.shape[2]), F32)
    summed = (
        jnp.concatenate([zero, taps[0][:-1]], axis=0)
        + taps[1]
        + jnp.concatenate([taps[2][1:], zero], axis=0)
    )
    hidden = jnp.maximum(summed, 0.0).astype(BF16)
    out_ref[...] = lax.dot_general(
        mask_ref[...], hidden, (((1,), (1,)), ((), ())), preferred_element_type=F32
    )

    for d in range(1, chips):
        query_copy(d)[0].wait_send()
        for copy in vals_copies(bit_xor(chip, d, chips)):
            copy.wait_send()
    for copy in sib_copies:
        copy.wait_send()
    q_sib.wait_send()
    r_sib.wait_send()

    @pl.when(has_other)
    def _():
        q_other.wait_send()
        r_other.wait_send()


def shards(
    mem_key,
    value_base,
    memory_labels,
    valid_counts,
    query_key,
    query_value,
    object_embed,
    decode_weight,
    mask_weight,
):
    n = lax.axis_size("mem")
    chips = n // 2
    key_width = mem_key.shape[2]
    val = value_base.shape[2]
    height, width = query_value.shape[:2]
    keys = mem_key.reshape(-1, key_width)
    base = value_base.reshape(-1, val)
    block = keys.shape[0]
    dec = decode_weight.shape[3]
    hbm = pl.BlockSpec(memory_space=pltpu.HBM)
    queries = query_key.reshape(-1, key_width)
    query_values = query_value.reshape(-1, val)
    mask = mask_weight.T
    staged = (keys, base, memory_labels, queries, query_values, object_embed, decode_weight, mask)
    dma = pltpu.SemaphoreType.DMA
    out = pl.pallas_call(
        functools.partial(kernel, n),
        out_shape=jax.ShapeDtypeStruct((mask_weight.shape[1], height * width), F32),
        in_specs=[pl.BlockSpec(memory_space=pltpu.SMEM)] + [hbm] * len(staged),
        out_specs=pl.BlockSpec(memory_space=pltpu.VMEM),
        scratch_shapes=[pltpu.VMEM(array.shape, array.dtype) for array in staged]
        + [
            dma((len(staged),)),
            pltpu.VMEM((block, val), BF16),
            pltpu.VMEM((block, key_width), BF16),
            pltpu.VMEM((block, val), BF16),
            pltpu.VMEM((8, block), F32),
            pltpu.VMEM((8, block), F32),
            pltpu.VMEM((chips, width, key_width), BF16),
            pltpu.VMEM((chips, width, val), BF16),
            pltpu.VMEM((chips // 2, 8, 2 * width), F32),
            pltpu.VMEM((chips, width, val), BF16),
            pltpu.VMEM((chips, 8, 2 * width), F32),
            pltpu.VMEM((2, width, val), BF16),
            pltpu.VMEM((2, width, val), BF16),
            pltpu.VMEM((width, val), BF16),
            pltpu.VMEM((3, width, dec), F32),
            dma((3,)),
            dma((3,)),
            dma((chips,)),
            dma((chips,)),
            dma((chips,)),
            dma((chips,)),
            dma((chips,)),
            dma((chips,)),
            dma((2,)),
            dma((2,)),
            dma((2,)),
            dma((2,)),
        ],
        compiler_params=pltpu.CompilerParams(
            collective_id=0, has_side_effects=True, vmem_limit_bytes=48 * 1024 * 1024
        ),
    )(valid_counts, *staged)
    return out.T.reshape(height, width, mask_weight.shape[1])


def solution(mesh):
    rows = ("groups", "mem")
    placed = (
        P(rows, None, None),
        P(rows, None, None),
        P(rows, None),
        P(rows),
        P(rows, None, None),
        P(rows, None, None),
        P(),
        P(),
        P(),
    )
    return jax.shard_map(
        shards,
        mesh=mesh,
        in_specs=placed,
        out_specs=P(rows, None, None),
        check_vma=False,
    )
```

```python
import functools
import math

import jax
import jax.numpy as jnp
from jax import lax
from jax.experimental import pallas as pl
from jax.experimental.pallas import tpu as pltpu
from jax.sharding import PartitionSpec as P

F32 = jnp.float32
BF16 = jnp.bfloat16


def bit_xor(a, b, size):
    out, bit = 0, 1
    while bit < size:
        out = out + ((a // bit + b // bit) % 2) * bit
        bit *= 2
    return out


def remote(src, dst, send, recv, target):
    return pltpu.make_async_remote_copy(
        src_ref=src,
        dst_ref=dst,
        send_sem=send,
        recv_sem=recv,
        device_id={"mem": target},
        device_id_type=pl.DeviceIdType.MESH,
    )


def kernel(
    n,
    count_ref,
    keys_hbm,
    base_hbm,
    labels_hbm,
    query_hbm,
    qval_hbm,
    embed_hbm,
    weight_hbm,
    mask_hbm,
    out_ref,
    keys_ref,
    base_ref,
    labels_ref,
    query_ref,
    qval_ref,
    embed_ref,
    weight,
    mask_ref,
    load_sem,
    values,
    sib_keys,
    sib_values,
    bias,
    sib_bias,
    queries,
    send_vals,
    send_stats,
    recv_vals,
    recv_stats,
    halo_q,
    halo_r,
    readout,
    acc,
    sib_send,
    sib_recv,
    query_send,
    query_recv,
    vals_send,
    vals_recv,
    stats_send,
    stats_recv,
    haloq_send,
    haloq_recv,
    halor_send,
    halor_recv,
):
    chips = n // 2
    zs = chips // 2
    me = lax.axis_index("mem")
    core = me % 2
    chip = me // 2
    y = chip % 2
    z = chip // 2
    sibling = me + 1 - 2 * core
    other = me - 1 + 2 * core
    has_other = jnp.logical_and(other >= 0, other < n)
    width, val = qval_ref.shape
    scale = 1.0 / math.sqrt(keys_ref.shape[1])

    barrier = pltpu.get_barrier_semaphore()

    def greet(target):
        pl.semaphore_signal(
            barrier, inc=1, device_id={"mem": target}, device_id_type=pl.DeviceIdType.MESH
        )

    greet(sibling)
    for d in range(1, chips):
        greet(bit_xor(chip, d, chips) * 2 + core)

    @pl.when(has_other)
    def _():
        greet(other)

    loads = [
        pltpu.make_async_copy(src, dst, load_sem.at[k])
        for k, (src, dst) in enumerate(
            (
                (query_hbm, query_ref),
                (labels_hbm, labels_ref),
                (embed_hbm, embed_ref),
                (base_hbm, base_ref),
                (keys_hbm, keys_ref),
                (qval_hbm, qval_ref),
                (mask_hbm, mask_ref),
                (weight_hbm, weight),
            )
        )
    ]
    for load in loads:
        load.start()
    for load in loads[:4]:
        load.wait()

    objects = embed_ref.shape[0]
    embed = embed_ref[...].astype(F32)
    cols = labels_ref.shape[1]
    for row in range(labels_ref.shape[0]):
        lab = jnp.broadcast_to(labels_ref[row : row + 1, :], (objects, cols))
        onehot = (lab == lax.broadcasted_iota(jnp.int32, (objects, cols), 0)).astype(F32)
        added = lax.dot_general(
            onehot, embed, (((0,), (0,)), ((), ())), preferred_element_type=F32
        )
        part = pl.ds(row * cols, cols)
        values[part, :] = (base_ref[part, :].astype(F32) + added).astype(BF16)
    place = lax.broadcasted_iota(jnp.int32, bias.shape, 1)
    bias[...] = jnp.where(place < count_ref[0], 0.0, -jnp.inf).astype(F32)
    queries[chip] = query_ref[...]

    for load in loads[4:6]:
        load.wait()
    pl.semaphore_wait(barrier, chips + has_other.astype(jnp.int32))

    def query_copy(d):
        peer = bit_xor(chip, d, chips)
        send = remote(
            query_ref, queries.at[chip], query_send.at[peer], query_recv.at[chip], peer * 2 + core
        )
        recv = remote(
            query_ref, queries.at[peer], query_send.at[peer], query_recv.at[peer], peer * 2 + core
        )
        return send, recv

    for d in range(chips - 1, 0, -1):
        query_copy(d)[0].start()
    sib_copies = [
        remote(src, dst, sib_send.at[k], sib_recv.at[k], sibling)
        for k, (src, dst) in enumerate(
            ((keys_ref, sib_keys), (bias, sib_bias), (values, sib_values))
        )
    ]
    for copy in sib_copies:
        copy.start()

    def halo_copies(src, buf, send, recv):
        to_sib = remote(src, buf.at[core], send.at[0], recv.at[core], sibling)
        from_sib = remote(src, buf.at[1 - core], send.at[0], recv.at[1 - core], sibling)
        to_other = remote(src, buf.at[1 - core], send.at[1], recv.at[1 - core], other)
        from_other = remote(src, buf.at[core], send.at[1], recv.at[core], other)
        return to_sib, from_sib, to_other, from_other

    q_sib, q_from_sib, q_other, q_from_other = halo_copies(qval_ref, halo_q, haloq_send, haloq_recv)
    q_sib.start()

    @pl.when(has_other)
    def _():
        q_other.start()

    @pl.when(jnp.logical_not(has_other))
    def _():
        halo_q[core] = jnp.zeros((width, val), BF16)
        halo_r[core] = jnp.zeros((width, val), BF16)

    def wait_query(target_chip):
        remote(
            query_ref,
            queries.at[target_chip],
            query_send.at[target_chip],
            query_recv.at[target_chip],
            target_chip * 2 + core,
        ).wait_recv()

    def vals_copies(target):
        return (
            remote(
                send_vals.at[target],
                recv_vals.at[chip],
                vals_send.at[target],
                vals_recv.at[chip],
                target * 2 + core,
            ),
            remote(
                send_stats.at[target // 2],
                recv_stats.at[chip],
                stats_send.at[target],
                stats_recv.at[chip],
                target * 2 + core,
            ),
        )

    def step(k, carry):
        d = zs - 1 - k
        zt = bit_xor(z, d, zs)
        for yt in range(2):

            @pl.when(zt * 2 + yt != chip)
            def _():
                wait_query(zt * 2 + yt)

        @pl.when(k == 0)
        def _():
            for copy in sib_copies:
                copy.wait_recv()

        q = queries[pl.ds(zt * 2, 2)].reshape(2 * width, -1)
        contract = (((1,), (1,)), ((), ()))
        s0 = lax.dot_general(q, keys_ref[...], contract, preferred_element_type=F32)
        s1 = lax.dot_general(q, sib_keys[...], contract, preferred_element_type=F32)
        s0 = s0 * scale + bias[0:1, :]
        s1 = s1 * scale + sib_bias[0:1, :]
        peak = jnp.maximum(
            jnp.max(s0, axis=1, keepdims=True), jnp.max(s1, axis=1, keepdims=True)
        )
        w0 = jnp.exp(s0 - peak).astype(BF16)
        w1 = jnp.exp(s1 - peak).astype(BF16)
        mass = jnp.sum(w0.astype(F32) + w1.astype(F32), axis=1, keepdims=True)
        summed = jnp.dot(w0, values[...], preferred_element_type=F32) + jnp.dot(
            w1, sib_values[...], preferred_element_type=F32
        )
        send_vals[pl.ds(zt * 2, 2)] = summed.astype(BF16).reshape(2, width, val)
        lane = lax.broadcasted_iota(jnp.int32, (2 * width, 128), 1)
        stats = jnp.where(lane == 0, peak, mass)
        send_stats[zt] = stats.T[0:8, :]
        for yt in range(2):
            target = zt * 2 + yt

            @pl.when(target != chip)
            def _():
                for copy in vals_copies(target):
                    copy.start()

        return carry

    lax.fori_loop(0, zs, step, 0)
    recv_vals[chip] = send_vals[chip]
    recv_stats[chip] = send_stats[z]

    for load in loads[6:]:
        load.wait()
    q_from_sib.wait_recv()

    @pl.when(has_other)
    def _():
        q_from_other.wait_recv()

    for dc in range(3):
        total = jnp.zeros((width, acc.shape[2]), F32)
        for dr, src in enumerate((halo_q.at[0], qval_ref, halo_q.at[1])):
            total += jnp.dot(src[...], weight[dr, dc, val:, :], preferred_element_type=F32)
        acc[dc] = total

    for d in range(1, chips):
        peer = bit_xor(chip, d, chips)
        remote(
            send_vals.at[peer], recv_vals.at[peer], vals_send.at[peer], vals_recv.at[peer],
            peer * 2 + core,
        ).wait_recv()
        remote(
            send_stats.at[peer // 2], recv_stats.at[peer], stats_send.at[peer],
            stats_recv.at[peer], peer * 2 + core,
        ).wait_recv()

    peaks, masses = [], []
    for first in range(0, chips, 16):
        tiles = recv_stats[first : min(first + 16, chips)].reshape(-1, 2 * width)
        have = tiles.shape[0] // 8
        tiles = jnp.concatenate([tiles] * (16 // have), axis=0)
        turned = tiles.T
        turned = jnp.where(y == 0, turned[:width], turned[width:])
        for k in range(have):
            peaks.append(turned[:, k * 8 : k * 8 + 1])
            masses.append(turned[:, k * 8 + 1 : k * 8 + 2])
    largest = functools.reduce(jnp.maximum, peaks)
    weight_sum = jnp.zeros((width, 1), F32)
    value_sum = jnp.zeros((width, val), F32)
    for k in range(chips):
        factor = jnp.exp(peaks[k] - largest)
        weight_sum += factor * masses[k]
        value_sum += factor * recv_vals[k].astype(F32)
    readout[...] = (value_sum / weight_sum).astype(BF16)

    r_sib, r_from_sib, r_other, r_from_other = halo_copies(readout, halo_r, halor_send, halor_recv)

    @pl.when(has_other)
    def _():
        r_other.start()

    r_sib.start()
    for dc in range(3):
        acc[dc] += jnp.dot(readout[...], weight[1, dc, :val, :], preferred_element_type=F32)
    r_from_sib.wait_recv()

    @pl.when(has_other)
    def _():
        r_from_other.wait_recv()

    taps = []
    for dc in range(3):
        total = acc[dc]
        for dr, slot in ((0, 0), (2, 1)):
            total += jnp.dot(halo_r[slot], weight[dr, dc, :val, :], preferred_element_type=F32)
        taps.append(total)
    zero = jnp.zeros((1, acc.shape[2]), F32)
    summed = (
        jnp.concatenate([zero, taps[0][:-1]], axis=0)
        + taps[1]
        + jnp.concatenate([taps[2][1:], zero], axis=0)
    )
    hidden = jnp.maximum(summed, 0.0).astype(BF16)
    out_ref[...] = lax.dot_general(
        mask_ref[...], hidden, (((1,), (1,)), ((), ())), preferred_element_type=F32
    )

    for d in range(1, chips):
        query_copy(d)[0].wait_send()
        for copy in vals_copies(bit_xor(chip, d, chips)):
            copy.wait_send()
    for copy in sib_copies:
        copy.wait_send()
    q_sib.wait_send()
    r_sib.wait_send()

    @pl.when(has_other)
    def _():
        q_other.wait_send()
        r_other.wait_send()


def shards(
    mem_key,
    value_base,
    memory_labels,
    valid_counts,
    query_key,
    query_value,
    object_embed,
    decode_weight,
    mask_weight,
):
    n = lax.axis_size("mem")
    chips = n // 2
    key_width = mem_key.shape[2]
    val = value_base.shape[2]
    height, width = query_value.shape[:2]
    keys = mem_key.reshape(-1, key_width)
    base = value_base.reshape(-1, val)
    block = keys.shape[0]
    dec = decode_weight.shape[3]
    hbm = pl.BlockSpec(memory_space=pltpu.HBM)
    queries = query_key.reshape(-1, key_width)
    query_values = query_value.reshape(-1, val)
    mask = mask_weight.T
    staged = (keys, base, memory_labels, queries, query_values, object_embed, decode_weight, mask)
    dma = pltpu.SemaphoreType.DMA
    out = pl.pallas_call(
        functools.partial(kernel, n),
        out_shape=jax.ShapeDtypeStruct((mask_weight.shape[1], height * width), F32),
        in_specs=[pl.BlockSpec(memory_space=pltpu.SMEM)] + [hbm] * len(staged),
        out_specs=pl.BlockSpec(memory_space=pltpu.VMEM),
        scratch_shapes=[pltpu.VMEM(array.shape, array.dtype) for array in staged]
        + [
            dma((len(staged),)),
            pltpu.VMEM((block, val), BF16),
            pltpu.VMEM((block, key_width), BF16),
            pltpu.VMEM((block, val), BF16),
            pltpu.VMEM((8, block), F32),
            pltpu.VMEM((8, block), F32),
            pltpu.VMEM((chips, width, key_width), BF16),
            pltpu.VMEM((chips, width, val), BF16),
            pltpu.VMEM((chips // 2, 8, 2 * width), F32),
            pltpu.VMEM((chips, width, val), BF16),
            pltpu.VMEM((chips, 8, 2 * width), F32),
            pltpu.VMEM((2, width, val), BF16),
            pltpu.VMEM((2, width, val), BF16),
            pltpu.VMEM((width, val), BF16),
            pltpu.VMEM((3, width, dec), F32),
            dma((3,)),
            dma((3,)),
            dma((chips,)),
            dma((chips,)),
            dma((chips,)),
            dma((chips,)),
            dma((chips,)),
            dma((chips,)),
            dma((2,)),
            dma((2,)),
            dma((2,)),
            dma((2,)),
        ],
        compiler_params=pltpu.CompilerParams(
            collective_id=0, has_side_effects=True, vmem_limit_bytes=60 * 1024 * 1024
        ),
    )(valid_counts, *staged)
    return out.T.reshape(height, width, mask_weight.shape[1])


def solution(mesh):
    rows = ("groups", "mem")
    placed = (
        P(rows, None, None),
        P(rows, None, None),
        P(rows, None),
        P(rows),
        P(rows, None, None),
        P(rows, None, None),
        P(),
        P(),
        P(),
    )
    return jax.shard_map(
        shards,
        mesh=mesh,
        in_specs=placed,
        out_specs=P(rows, None, None),
        check_vma=False,
    )
```

```python
import functools
import math

import jax
import jax.numpy as jnp
from jax import lax
from jax.experimental import pallas as pl
from jax.experimental.pallas import tpu as pltpu
from jax.sharding import PartitionSpec as P

F32 = jnp.float32
BF16 = jnp.bfloat16


def bit_xor(a, b, size):
    out, bit = 0, 1
    while bit < size:
        out = out + ((a // bit + b // bit) % 2) * bit
        bit *= 2
    return out


def remote(src, dst, send, recv, target):
    return pltpu.make_async_remote_copy(
        src_ref=src,
        dst_ref=dst,
        send_sem=send,
        recv_sem=recv,
        device_id={"mem": target},
        device_id_type=pl.DeviceIdType.MESH,
    )


def kernel(
    n,
    count_ref,
    keys_hbm,
    base_hbm,
    labels_hbm,
    query_hbm,
    qval_hbm,
    embed_hbm,
    weight_hbm,
    mask_hbm,
    out_ref,
    keys_ref,
    base_ref,
    labels_ref,
    query_ref,
    qval_ref,
    embed_ref,
    weight,
    mask_ref,
    load_sem,
    values,
    sib_keys,
    sib_values,
    bias,
    sib_bias,
    queries,
    own_vals,
    own_stats,
    send_y,
    recv_y,
    y_stats,
    send_vals,
    send_stats,
    recv_vals,
    recv_stats,
    halo_q,
    halo_r,
    readout,
    acc,
    sib_send,
    sib_recv,
    query_send,
    query_recv,
    y_send,
    y_recv,
    ys_send,
    ys_recv,
    vals_send,
    vals_recv,
    stats_send,
    stats_recv,
    haloq_send,
    haloq_recv,
    halor_send,
    halor_recv,
):
    chips = n // 2
    zs = chips // 2
    me = lax.axis_index("mem")
    core = me % 2
    chip = me // 2
    y = chip % 2
    z = chip // 2
    sibling = me + 1 - 2 * core
    other = me - 1 + 2 * core
    has_other = jnp.logical_and(other >= 0, other < n)
    width, val = qval_ref.shape
    scale = 1.0 / math.sqrt(keys_ref.shape[1])

    barrier = pltpu.get_barrier_semaphore()

    def greet(target):
        pl.semaphore_signal(
            barrier, inc=1, device_id={"mem": target}, device_id_type=pl.DeviceIdType.MESH
        )

    greet(sibling)
    for d in range(1, chips):
        greet(bit_xor(chip, d, chips) * 2 + core)

    @pl.when(has_other)
    def _():
        greet(other)

    loads = [
        pltpu.make_async_copy(src, dst, load_sem.at[k])
        for k, (src, dst) in enumerate(
            (
                (query_hbm, query_ref),
                (labels_hbm, labels_ref),
                (embed_hbm, embed_ref),
                (base_hbm, base_ref),
                (keys_hbm, keys_ref),
                (qval_hbm, qval_ref),
                (mask_hbm, mask_ref),
                (weight_hbm, weight),
            )
        )
    ]
    for load in loads:
        load.start()
    for load in loads[:4]:
        load.wait()

    objects = embed_ref.shape[0]
    embed = embed_ref[...].astype(F32)
    cols = labels_ref.shape[1]
    for row in range(labels_ref.shape[0]):
        lab = jnp.broadcast_to(labels_ref[row : row + 1, :], (objects, cols))
        onehot = (lab == lax.broadcasted_iota(jnp.int32, (objects, cols), 0)).astype(F32)
        added = lax.dot_general(
            onehot, embed, (((0,), (0,)), ((), ())), preferred_element_type=F32
        )
        part = pl.ds(row * cols, cols)
        values[part, :] = (base_ref[part, :].astype(F32) + added).astype(BF16)
    place = lax.broadcasted_iota(jnp.int32, bias.shape, 1)
    bias[...] = jnp.where(place < count_ref[0], 0.0, -jnp.inf).astype(F32)
    queries[chip] = query_ref[...]

    for load in loads[4:6]:
        load.wait()
    pl.semaphore_wait(barrier, chips + has_other.astype(jnp.int32))

    def query_copy(d):
        peer = bit_xor(chip, d, chips)
        send = remote(
            query_ref, queries.at[chip], query_send.at[peer], query_recv.at[chip], peer * 2 + core
        )
        recv = remote(
            query_ref, queries.at[peer], query_send.at[peer], query_recv.at[peer], peer * 2 + core
        )
        return send, recv

    for d in range(chips - 1, 0, -1):
        query_copy(d)[0].start()
    sib_copies = [
        remote(src, dst, sib_send.at[k], sib_recv.at[k], sibling)
        for k, (src, dst) in enumerate(
            ((keys_ref, sib_keys), (bias, sib_bias), (values, sib_values))
        )
    ]
    for copy in sib_copies:
        copy.start()

    def halo_copies(src, buf, send, recv):
        to_sib = remote(src, buf.at[core], send.at[0], recv.at[core], sibling)
        from_sib = remote(src, buf.at[1 - core], send.at[0], recv.at[1 - core], sibling)
        to_other = remote(src, buf.at[1 - core], send.at[1], recv.at[1 - core], other)
        from_other = remote(src, buf.at[core], send.at[1], recv.at[core], other)
        return to_sib, from_sib, to_other, from_other

    q_sib, q_from_sib, q_other, q_from_other = halo_copies(qval_ref, halo_q, haloq_send, haloq_recv)
    q_sib.start()

    @pl.when(has_other)
    def _():
        q_other.start()

    @pl.when(jnp.logical_not(has_other))
    def _():
        halo_q[core] = jnp.zeros((width, val), BF16)
        halo_r[core] = jnp.zeros((width, val), BF16)

    def wait_query(target_chip):
        remote(
            query_ref,
            queries.at[target_chip],
            query_send.at[target_chip],
            query_recv.at[target_chip],
            target_chip * 2 + core,
        ).wait_recv()

    y_peer = chip + 1 - 2 * y

    def y_copies(zt):
        return (
            remote(
                send_y.at[zt], recv_y.at[zt], y_send.at[zt], y_recv.at[zt], y_peer * 2 + core
            ),
            remote(
                own_stats.at[zt],
                y_stats.at[zt],
                ys_send.at[zt],
                ys_recv.at[zt],
                y_peer * 2 + core,
            ),
        )

    def z_copies(zt, slot):
        target = (zt * 2 + y) * 2 + core
        return (
            remote(
                send_vals.at[zt], recv_vals.at[slot], vals_send.at[zt], vals_recv.at[slot], target
            ),
            remote(
                send_stats.at[zt],
                recv_stats.at[slot],
                stats_send.at[zt],
                stats_recv.at[slot],
                target,
            ),
        )

    def attend(k, carry):
        zt = bit_xor(z, zs - 1 - k, zs)
        for yt in range(2):

            @pl.when(zt * 2 + yt != chip)
            def _():
                wait_query(zt * 2 + yt)

        @pl.when(k == 0)
        def _():
            for copy in sib_copies:
                copy.wait_recv()

        q = queries[pl.ds(zt * 2, 2)].reshape(2 * width, -1)
        contract = (((1,), (1,)), ((), ()))
        s0 = lax.dot_general(q, keys_ref[...], contract, preferred_element_type=F32)
        s1 = lax.dot_general(q, sib_keys[...], contract, preferred_element_type=F32)
        s0 = s0 * scale + bias[0:1, :]
        s1 = s1 * scale + sib_bias[0:1, :]
        peak = jnp.maximum(
            jnp.max(s0, axis=1, keepdims=True), jnp.max(s1, axis=1, keepdims=True)
        )
        w0 = jnp.exp(s0 - peak).astype(BF16)
        w1 = jnp.exp(s1 - peak).astype(BF16)
        mass = jnp.sum(w0.astype(F32) + w1.astype(F32), axis=1, keepdims=True)
        summed = jnp.dot(w0, values[...], preferred_element_type=F32) + jnp.dot(
            w1, sib_values[...], preferred_element_type=F32
        )
        own_vals[zt] = jnp.where(y == 0, summed[:width], summed[width:])
        send_y[zt] = jnp.where(y == 0, summed[width:], summed[:width]).astype(BF16)
        lane = lax.broadcasted_iota(jnp.int32, (2 * width, 128), 1)
        stats = jnp.where(lane == 0, peak, mass)
        own_stats[zt] = stats.T[0:8, :]
        for copy in y_copies(zt):
            copy.start()
        return carry

    lax.fori_loop(0, zs, attend, 0)

    def merge(k, carry):
        zt = bit_xor(z, zs - 1 - k, zs)
        for copy in y_copies(zt):
            copy.wait_recv()
        mine, theirs = own_stats[zt], y_stats[zt]
        turned = jnp.concatenate([mine, theirs] * (width // 8), axis=0).T
        turned = jnp.where(y == 0, turned[:width], turned[width:])
        mine_peak, theirs_peak = turned[:, 0:1], turned[:, 8:9]
        peak = jnp.maximum(mine_peak, theirs_peak)
        merged = (
            jnp.exp(mine_peak - peak) * own_vals[zt]
            + jnp.exp(theirs_peak - peak) * recv_y[zt].astype(F32)
        ).astype(BF16)
        top = jnp.maximum(mine[0:1], theirs[0:1])
        mass = jnp.exp(mine[0:1] - top) * mine[1:2] + jnp.exp(theirs[0:1] - top) * theirs[1:2]
        sub = lax.broadcasted_iota(jnp.int32, mine.shape, 0)
        stats = jnp.where(sub == 0, top, mass)

        @pl.when(zt != z)
        def _():
            send_vals[zt] = merged
            send_stats[zt] = stats
            for copy in z_copies(zt, z):
                copy.start()

        @pl.when(zt == z)
        def _():
            recv_vals[z] = merged
            recv_stats[z] = stats

        return carry

    lax.fori_loop(0, zs, merge, 0)

    for load in loads[6:]:
        load.wait()
    q_from_sib.wait_recv()

    @pl.when(has_other)
    def _():
        q_from_other.wait_recv()

    for dc in range(3):
        total = jnp.zeros((width, acc.shape[2]), F32)
        for dr, src in enumerate((halo_q.at[0], qval_ref, halo_q.at[1])):
            total += jnp.dot(src[...], weight[dr, dc, val:, :], preferred_element_type=F32)
        acc[dc] = total

    for d in range(1, zs):
        peer = bit_xor(z, d, zs)
        for copy in z_copies(peer, peer):
            copy.wait_recv()

    peaks, masses = [], []
    for first in range(0, zs, 16):
        tiles = recv_stats[first : min(first + 16, zs)].reshape(-1, 2 * width)
        have = tiles.shape[0] // 8
        tiles = jnp.concatenate([tiles] * (16 // have), axis=0)
        turned = tiles.T
        turned = jnp.where(y == 0, turned[:width], turned[width:])
        for k in range(have):
            peaks.append(turned[:, k * 8 : k * 8 + 1])
            masses.append(turned[:, k * 8 + 1 : k * 8 + 2])
    largest = functools.reduce(jnp.maximum, peaks)
    weight_sum = jnp.zeros((width, 1), F32)
    value_sum = jnp.zeros((width, val), F32)
    for k in range(zs):
        factor = jnp.exp(peaks[k] - largest)
        weight_sum += factor * masses[k]
        value_sum += factor * recv_vals[k].astype(F32)
    readout[...] = (value_sum / weight_sum).astype(BF16)

    r_sib, r_from_sib, r_other, r_from_other = halo_copies(readout, halo_r, halor_send, halor_recv)

    @pl.when(has_other)
    def _():
        r_other.start()

    r_sib.start()
    for dc in range(3):
        acc[dc] += jnp.dot(readout[...], weight[1, dc, :val, :], preferred_element_type=F32)
    r_from_sib.wait_recv()

    @pl.when(has_other)
    def _():
        r_from_other.wait_recv()

    taps = []
    for dc in range(3):
        total = acc[dc]
        for dr, slot in ((0, 0), (2, 1)):
            total += jnp.dot(halo_r[slot], weight[dr, dc, :val, :], preferred_element_type=F32)
        taps.append(total)
    zero = jnp.zeros((1, acc.shape[2]), F32)
    summed = (
        jnp.concatenate([zero, taps[0][:-1]], axis=0)
        + taps[1]
        + jnp.concatenate([taps[2][1:], zero], axis=0)
    )
    hidden = jnp.maximum(summed, 0.0).astype(BF16)
    out_ref[...] = lax.dot_general(
        mask_ref[...], hidden, (((1,), (1,)), ((), ())), preferred_element_type=F32
    )

    for d in range(1, chips):
        query_copy(d)[0].wait_send()
    for d in range(zs):
        peer = bit_xor(z, d, zs)
        for copy in y_copies(peer) + (z_copies(peer, z) if d else ()):
            copy.wait_send()
    for copy in sib_copies:
        copy.wait_send()
    q_sib.wait_send()
    r_sib.wait_send()

    @pl.when(has_other)
    def _():
        q_other.wait_send()
        r_other.wait_send()


def shards(
    mem_key,
    value_base,
    memory_labels,
    valid_counts,
    query_key,
    query_value,
    object_embed,
    decode_weight,
    mask_weight,
):
    n = lax.axis_size("mem")
    chips = n // 2
    zs = chips // 2
    key_width = mem_key.shape[2]
    val = value_base.shape[2]
    height, width = query_value.shape[:2]
    keys = mem_key.reshape(-1, key_width)
    base = value_base.reshape(-1, val)
    block = keys.shape[0]
    dec = decode_weight.shape[3]
    hbm = pl.BlockSpec(memory_space=pltpu.HBM)
    queries = query_key.reshape(-1, key_width)
    query_values = query_value.reshape(-1, val)
    mask = mask_weight.T
    staged = (keys, base, memory_labels, queries, query_values, object_embed, decode_weight, mask)
    dma = pltpu.SemaphoreType.DMA
    out = pl.pallas_call(
        functools.partial(kernel, n),
        out_shape=jax.ShapeDtypeStruct((mask_weight.shape[1], height * width), F32),
        in_specs=[pl.BlockSpec(memory_space=pltpu.SMEM)] + [hbm] * len(staged),
        out_specs=pl.BlockSpec(memory_space=pltpu.VMEM),
        scratch_shapes=[pltpu.VMEM(array.shape, array.dtype) for array in staged]
        + [
            dma((len(staged),)),
            pltpu.VMEM((block, val), BF16),
            pltpu.VMEM((block, key_width), BF16),
            pltpu.VMEM((block, val), BF16),
            pltpu.VMEM((8, block), F32),
            pltpu.VMEM((8, block), F32),
            pltpu.VMEM((chips, width, key_width), BF16),
            pltpu.VMEM((zs, width, val), F32),
            pltpu.VMEM((zs, 8, 2 * width), F32),
            pltpu.VMEM((zs, width, val), BF16),
            pltpu.VMEM((zs, width, val), BF16),
            pltpu.VMEM((zs, 8, 2 * width), F32),
            pltpu.VMEM((zs, width, val), BF16),
            pltpu.VMEM((zs, 8, 2 * width), F32),
            pltpu.VMEM((zs, width, val), BF16),
            pltpu.VMEM((zs, 8, 2 * width), F32),
            pltpu.VMEM((2, width, val), BF16),
            pltpu.VMEM((2, width, val), BF16),
            pltpu.VMEM((width, val), BF16),
            pltpu.VMEM((3, width, dec), F32),
            dma((3,)),
            dma((3,)),
            dma((chips,)),
            dma((chips,)),
            dma((zs,)),
            dma((zs,)),
            dma((zs,)),
            dma((zs,)),
            dma((zs,)),
            dma((zs,)),
            dma((zs,)),
            dma((zs,)),
            dma((2,)),
            dma((2,)),
            dma((2,)),
            dma((2,)),
        ],
        compiler_params=pltpu.CompilerParams(
            collective_id=0, has_side_effects=True, vmem_limit_bytes=60 * 1024 * 1024
        ),
    )(valid_counts, *staged)
    return out.T.reshape(height, width, mask_weight.shape[1])


def solution(mesh):
    rows = ("groups", "mem")
    placed = (
        P(rows, None, None),
        P(rows, None, None),
        P(rows, None),
        P(rows),
        P(rows, None, None),
        P(rows, None, None),
        P(),
        P(),
        P(),
    )
    return jax.shard_map(
        shards,
        mesh=mesh,
        in_specs=placed,
        out_specs=P(rows, None, None),
        check_vma=False,
    )
```
